512 devices in a mesh: section: 16 (over z_lo, x), dp: 32 (over z_hi, y, core).
Axes of the slice: x: 4, y: 4, z: 16 (z_hi: 4, z_lo: 4; z = z_hi * 4 + z_lo), core: 2. Of those that a mesh axis runs over, the one named last changes fastest.
Arguments:
- enc_out: bfloat16 [1024, 6144], P('dp'), may hold values from -6 to 6
- kv_weight: bfloat16 [16, 6144, 256], P('section', 'dp'), may hold values from -0.078125 to 0.078125
- queries: bfloat16 [16, 16384, 128], P('section', 'dp'), may hold values from -128 to 128
- out_grad: bfloat16 [16, 16384, 128], P('section', 'dp'), may hold values from -6 to 6
Outputs:
- enc_grad: bfloat16 [16, 1024, 6144], P('section', 'dp')
- weight_grad: float32 [16, 6144, 256], P('section', 'dp')
The draws below stay inside these ranges and needn't reach their ends.
All inputs are finite; a program needn't handle non-finite values.
Results may differ from the reference program's by a relative error of at most 0.025.
The reference program's roundings to bfloat16 on the way count: a program that leaves them out, or rounds other values in their place, can miss the bound.
Values may be sent and summed in bfloat16 or wider, within the bound.
No kernel may reach another device: no remote copies, remote signals or barrier semaphores. Data moves between devices by JAX's collectives and lax.ppermute only.
A program may use at most 64 MiB of HBM per device.

```python
import jax
import jax.numpy as jnp
from jax import lax

D = 6144
DH = 128
ENC_DEV = 32
DEC_DEV = 512
SECTIONS = 16
ENC_TOK = 1024
DEC_TOK = 16384
N_DP = 32


def draw_queries(key, part):
    key = jax.random.fold_in(key, 7)
    base = jnp.clip(jax.random.normal(key, (SECTIONS, DEC_TOK, DH), jnp.float32), -6.0, 6.0)
    return base.astype(jnp.bfloat16)


def raised(array, own_key, source, target, parts, factor):
    def block_of(dim):
        return (jnp.arange(array.shape[dim]) // (array.shape[dim] // parts)).reshape((-1,) + (1,) * (array.ndim - 1 - dim))

    near = jax.random.permutation(own_key, parts)[block_of(target)]
    other_side = (block_of(target) + parts // 2) % parts
    return jnp.where((block_of(source) == near) | (block_of(source) == other_side), factor * array, array)


def shard_levels(stream_key, dims, shards, low, high):
    loudness, own = 1.0, jax.random.fold_in(stream_key, 6)
    for position, shards_of in shards:
        heights = jnp.exp(jax.random.uniform(jax.random.fold_in(own, position), (shards_of,), jnp.float32, low / len(shards), high / len(shards)))
        loudness = loudness * jnp.repeat(heights, dims[position] // shards_of).reshape([-1 if axis == position else 1 for axis in range(len(dims))])
    return loudness


def normal_values(own_key, shape, scale, bound, split=(), held_as=jnp.bfloat16):
    entries = jax.random.normal(own_key, shape, jnp.float32) * scale
    if len(split) > 0:
        entries = shard_levels(own_key, shape, split, -0.22, 0.18) * entries
    return jnp.clip(entries, min=-bound, max=bound).astype(held_as)


def noise_with(own_key, dims, width, bound, pieces, heavy, held_as=jnp.bfloat16):
    entries = width * jax.random.normal(own_key, dims, jnp.float32)
    if pieces:
        entries = entries * shard_levels(own_key, dims, pieces, -0.22, 0.18)
    return jnp.clip(raised(entries, jax.random.fold_in(own_key, 3), *heavy), -bound, bound).astype(held_as)


def setup_inputs(seed: int = 0) -> dict:
    arg_keys = jax.random.split(jax.random.key(seed), 5)
    return {
        "enc_out": noise_with(arg_keys[0], (ENC_TOK, D), 1.0, 6.0, ((0, 32),), (0, 1, 32, 2.75)),
        "kv_weight": normal_values(arg_keys[1], (SECTIONS, D, 2 * DH), D ** -0.5, 0.078125, ((0, 16), (1, 32))),
        "queries": draw_queries(jax.random.fold_in(arg_keys[4], 71), 0),
        "out_grad": normal_values(arg_keys[3], (SECTIONS, DEC_TOK, DH), 1.0, 6.0, ((0, 16), (1, 32))),
    }


def reference(enc_out, kv_weight, queries, out_grad):
    logit_scale = 1.0 / (DH ** 0.5)
    enc_blocks = enc_out.reshape(N_DP, ENC_DEV, D).astype(jnp.float32)

    def layer(carry, index):
        weights = kv_weight[index]
        kv_low = jnp.dot(enc_out, weights, preferred_element_type=jnp.float32).astype(jnp.bfloat16)
        kv_blocks = kv_low.reshape(N_DP, ENC_DEV, 2 * DH).astype(jnp.float32)
        encoder_keys = kv_blocks[:, :, :DH]
        encoder_values = kv_blocks[:, :, DH:]
        decoder_query = queries[index].reshape(N_DP, DEC_DEV, DH).astype(jnp.float32)
        upstream_gradient = out_grad[index].reshape(N_DP, DEC_DEV, DH).astype(jnp.float32)
        attention_scores = jnp.einsum("fjg,fdg->fjd", decoder_query, encoder_keys) * logit_scale
        peak = jnp.max(attention_scores, axis=-1, keepdims=True)
        expd = jnp.exp(attention_scores - peak)
        probs = expd / jnp.sum(expd, axis=-1, keepdims=True)
        probabilities_reduced = probs.astype(jnp.bfloat16).astype(jnp.float32)
        probability_gradient = jnp.einsum("fjg,fdg->fjd", upstream_gradient, encoder_values)
        delta = jnp.sum(probs * probability_gradient, axis=-1, keepdims=True)
        score_gradient = (probs * (probability_gradient - delta) * logit_scale).astype(jnp.bfloat16).astype(jnp.float32)
        key_gradient = jnp.einsum("nzu,nzs->nus", score_gradient, decoder_query)
        value_gradient = jnp.einsum("nzu,nzs->nus", probabilities_reduced, upstream_gradient)
        dkv = jnp.concatenate([key_gradient, value_gradient], axis=-1).astype(jnp.bfloat16)
        partial_value = lax.dot_general(dkv.reshape(ENC_TOK, 2 * DH), weights, (((1,), (1,)), ((), ())), preferred_element_type=jnp.float32)
        total = carry + partial_value
        terms = jnp.einsum("bed,bek->bdk", enc_blocks, dkv.astype(jnp.float32))
        grad = jnp.sum(terms.astype(jnp.bfloat16).astype(jnp.float32), axis=0)
        return total, (total.astype(jnp.bfloat16), grad)

    start = jnp.zeros((ENC_TOK, D), jnp.float32)
    final, outputs = lax.scan(layer, start, jnp.arange(SECTIONS), reverse=True)
    return outputs[0], outputs[1]
```

```python
import functools

import jax
import jax.numpy as jnp
from jax import lax
from jax.experimental import pallas as pl
from jax.experimental.pallas import tpu as pltpu
from jax.sharding import PartitionSpec as P

Z_HI = 4
NEAR = 8


def contract(left, right, left_dim, right_dim):
    return lax.dot_general(
        left, right, (((left_dim,), (right_dim,)), ((), ())), preferred_element_type=jnp.float32
    )


def split_columns(enc_ref, out_ref):
    width = out_ref.shape[2] // Z_HI
    for near in range(NEAR):
        for far in range(Z_HI):
            start = (far * NEAR + near) * width
            out_ref[near, :, far * width : (far + 1) * width] = enc_ref[:, start : start + width]


def join_columns(in_ref, out_ref):
    width = in_ref.shape[2] // Z_HI
    for near in range(NEAR):
        for far in range(Z_HI):
            start = (far * NEAR + near) * width
            out_ref[0, :, start : start + width] = in_ref[near, :, far * width : (far + 1) * width]


def project(place_ref, own_ref, one_ref, two_ref, three_ref, enc_ref, weights_ref, kv_ref):
    place = place_ref[0]
    depth = own_ref.shape[0]
    for step, ref in enumerate((own_ref, one_ref, two_ref, three_ref)):
        far = lax.rem(place + Z_HI - step, Z_HI)
        weights_ref[pl.ds(pl.multiple_of(far * depth, depth), depth), :] = ref[...]
    near, rows, width = enc_ref.shape
    enc = enc_ref[...].reshape(near * rows, width)
    kv = jnp.dot(enc, weights_ref[...], preferred_element_type=jnp.float32)
    kv_ref[...] = kv.reshape(near, rows, kv.shape[1])


def attend(kv_ref, queries_ref, grad_ref, dkv_ref):
    kv = kv_ref[0]
    for near in range(1, kv_ref.shape[0]):
        kv = kv + kv_ref[near]
    kv = kv.astype(jnp.bfloat16)
    head = queries_ref.shape[1]
    scale = 1.0 / head**0.5
    queries = queries_ref[...]
    grad = grad_ref[...]
    scores = contract(kv[:, :head], queries, 1, 1) * scale
    expd = jnp.exp(scores - jnp.max(scores, axis=0, keepdims=True))
    probs = expd / jnp.sum(expd, axis=0, keepdims=True)
    dprobs = contract(kv[:, head:], grad, 1, 1)
    delta = jnp.sum(probs * dprobs, axis=0, keepdims=True)
    dscores = (probs * (dprobs - delta) * scale).astype(jnp.bfloat16)
    dkv_ref[:, :head] = contract(dscores, queries, 1, 0).astype(jnp.bfloat16)
    dkv_ref[:, head:] = contract(probs.astype(jnp.bfloat16), grad, 1, 0).astype(jnp.bfloat16)


def spread(dkv_ref, weights_ref, out_ref):
    near, rows, width = dkv_ref.shape
    dkv = dkv_ref[...].reshape(near * rows, width)
    out = contract(dkv, weights_ref[...], 1, 1)
    out_ref[...] = out.astype(jnp.bfloat16).reshape(out_ref.shape)


def weight_terms(enc_ref, dkv_ref, out_ref):
    near, rows, width = dkv_ref.shape
    dkv = dkv_ref[...].reshape(near * rows, width)
    enc = enc_ref[...].reshape(near * rows, enc_ref.shape[2])
    out_ref[...] = contract(enc, dkv, 0, 0).astype(jnp.bfloat16).reshape(out_ref.shape)


def suffix_sums(in_ref, out_ref):
    sections = in_ref.shape[0]
    total = in_ref[sections - 1].astype(jnp.float32)
    out_ref[sections - 1] = in_ref[sections - 1]
    for section in range(sections - 2, -1, -1):
        total = total + in_ref[section].astype(jnp.float32)
        out_ref[section] = total.astype(jnp.bfloat16)


def add_terms(in_ref, out_ref):
    total = in_ref[0].astype(jnp.float32)
    for far in range(1, in_ref.shape[0]):
        total = total + in_ref[far].astype(jnp.float32)
    out_ref[0] = total


def call(kernel, shape, dtype, args, flops=0, scalars=0):
    many = isinstance(dtype, tuple)
    outs = [jax.ShapeDtypeStruct(s, d) for s, d in zip(shape, dtype)] if many else jax.ShapeDtypeStruct(shape, dtype)
    vmem = pl.BlockSpec(memory_space=pltpu.VMEM)
    smem = pl.BlockSpec(memory_space=pltpu.SMEM)
    moved = sum(a.size * a.dtype.itemsize for a in args) + sum(o.size * o.dtype.itemsize for o in (outs if many else [outs]))
    return pl.pallas_call(
        kernel,
        out_shape=outs,
        in_specs=[smem] * scalars + [vmem] * (len(args) - scalars),
        out_specs=[vmem] * len(outs) if many else vmem,
        cost_estimate=pl.CostEstimate(flops=flops, bytes_accessed=moved, transcendentals=0),
        compiler_params=pltpu.CompilerParams(vmem_limit_bytes=24 << 20),
    )(*args)


def shards(enc_out, kv_weight, queries, out_grad):
    rows, model = enc_out.shape
    depth, both = kv_weight.shape[1:]
    sections = lax.axis_size("section")
    width = Z_HI * depth
    near_groups = [[far * NEAR + near for near in range(NEAR)] for far in range(Z_HI)]
    far_groups = [[far * NEAR + near for far in range(Z_HI)] for near in range(NEAR)]
    place = (lax.axis_index("dp") // NEAR).astype(jnp.int32).reshape(1)
    own = kv_weight[0]

    def shifted(step):
        pairs = [
            (far * NEAR + near, (far + step) % Z_HI * NEAR + near) for far in range(Z_HI) for near in range(NEAR)
        ]
        return lax.ppermute(own, "dp", pairs)

    def exchange(array, axis, groups=None):
        return lax.all_to_all(array, axis, 0, 0, axis_index_groups=groups)

    others = [shifted(step) for step in (1, 2, 3)]
    enc = call(split_columns, (NEAR, rows, width), jnp.bfloat16, [enc_out])
    enc = exchange(enc, "dp", near_groups)
    weights, kv = call(
        project,
        ((width, both), (NEAR, rows, both)),
        (jnp.bfloat16, jnp.float32),
        [place, own, *others, enc],
        flops=2 * NEAR * rows * width * both,
        scalars=1,
    )
    kv = exchange(kv, "dp", near_groups)
    dkv = call(attend, (rows, both), jnp.bfloat16, [kv, queries[0], out_grad[0]], flops=8 * rows * queries.size)
    dkv = exchange(jnp.broadcast_to(dkv[None], (NEAR, rows, both)), "dp", near_groups)
    piece = NEAR * rows // sections
    part = call(
        spread, (sections, piece, width), jnp.bfloat16, [dkv, weights], flops=2 * NEAR * rows * width * both
    )
    part = exchange(part, "section")
    terms = call(
        weight_terms, (Z_HI, depth, both), jnp.bfloat16, [enc, dkv], flops=2 * NEAR * rows * width * both
    )
    terms = exchange(terms, "dp", far_groups)
    sums = call(suffix_sums, (sections, piece, width), jnp.bfloat16, [part])
    sums = exchange(sums, "section")
    sums = exchange(sums.reshape(NEAR, rows, width), "dp", near_groups)
    enc_grad = call(join_columns, (1, rows, model), jnp.bfloat16, [sums])
    weight_grad = call(add_terms, (1, depth, both), jnp.float32, [terms])
    return enc_grad, weight_grad


def solution(mesh):
    in_specs = (
        P("dp", None),
        P("section", "dp", None),
        P("section", "dp", None),
        P("section", "dp", None),
    )
    out_specs = (P("section", "dp", None), P("section", "dp", None))
    return jax.shard_map(shards, mesh=mesh, in_specs=in_specs, out_specs=out_specs, check_vma=False)
```

```python
import jax
import jax.numpy as jnp
from jax import lax
from jax.experimental import pallas as pl
from jax.experimental.pallas import tpu as pltpu
from jax.sharding import PartitionSpec as P

Z_HI = 4
Z_LO = 4
NEAR = 8


def contract(left, right, left_dim, right_dim):
    return lax.dot_general(
        left, right, (((left_dim,), (right_dim,)), ((), ())), preferred_element_type=jnp.float32
    )


def split_columns(enc_ref, out_ref):
    width = out_ref.shape[2] // Z_HI
    for near in range(NEAR):
        for far in range(Z_HI):
            start = (far * NEAR + near) * width
            out_ref[near, :, far * width : (far + 1) * width] = enc_ref[:, start : start + width]


def join_columns(in_ref, out_ref):
    width = in_ref.shape[2] // Z_HI
    for near in range(NEAR):
        for far in range(Z_HI):
            start = (far * NEAR + near) * width
            out_ref[0, :, start : start + width] = in_ref[near, :, far * width : (far + 1) * width]


def project(enc_ref, weights_ref, kv_ref):
    near, rows, width = enc_ref.shape
    enc = enc_ref[...].reshape(near * rows, width)
    kv = jnp.dot(enc, weights_ref[...], preferred_element_type=jnp.float32)
    kv_ref[...] = kv.reshape(near, rows, kv.shape[1])


def attend(kv_ref, queries_ref, grad_ref, dkv_ref):
    kv = kv_ref[0]
    for near in range(1, kv_ref.shape[0]):
        kv = kv + kv_ref[near]
    kv = kv.astype(jnp.bfloat16)
    head = queries_ref.shape[1]
    scale = 1.0 / head**0.5
    queries = queries_ref[...]
    grad = grad_ref[...]
    scores = contract(kv[:, :head], queries, 1, 1) * scale
    expd = jnp.exp(scores - jnp.max(scores, axis=0, keepdims=True))
    probs = expd / jnp.sum(expd, axis=0, keepdims=True)
    dprobs = contract(kv[:, head:], grad, 1, 1)
    delta = jnp.sum(probs * dprobs, axis=0, keepdims=True)
    dscores = (probs * (dprobs - delta) * scale).astype(jnp.bfloat16)
    dkv_ref[:, :head] = contract(dscores, queries, 1, 0).astype(jnp.bfloat16)
    dkv_ref[:, head:] = contract(probs.astype(jnp.bfloat16), grad, 1, 0).astype(jnp.bfloat16)


def spread(dkv_ref, weights_ref, out_ref):
    near, rows, width = dkv_ref.shape
    dkv = dkv_ref[...].reshape(near * rows, width)
    out = contract(dkv, weights_ref[...], 1, 1)
    out_ref[...] = out.astype(jnp.bfloat16).reshape(out_ref.shape)


def weight_terms(place_ref, enc_ref, dkv_ref, own_ref, next_ref, far_ref, last_ref, terms_ref):
    near, rows, width = dkv_ref.shape
    dkv = dkv_ref[...].reshape(near * rows, width)
    enc = enc_ref[...].reshape(near * rows, enc_ref.shape[2])
    terms = contract(enc, dkv, 0, 0)
    depth = own_ref.shape[0]
    for far in range(Z_HI):
        terms_ref[far] = terms[far * depth : (far + 1) * depth]
    for step, ref in enumerate((own_ref, next_ref, far_ref, last_ref)):
        ref[...] = terms_ref[lax.rem(place_ref[0] + step, Z_HI)].astype(ref.dtype)


def row_total(in_ref, out_ref):
    total = in_ref[0].astype(jnp.float32)
    for step in range(1, in_ref.shape[0]):
        total = total + in_ref[step].astype(jnp.float32)
    out_ref[...] = total.astype(jnp.bfloat16)


def suffix_sums(in_ref, one_ref, two_ref, three_ref, out_ref):
    total = one_ref[...].astype(jnp.float32) + two_ref[...].astype(jnp.float32) + three_ref[...].astype(jnp.float32)
    for step in range(in_ref.shape[0] - 1, -1, -1):
        total = total + in_ref[step].astype(jnp.float32)
        out_ref[step] = total.astype(jnp.bfloat16)


def add_terms(own_ref, *refs):
    total = own_ref[...]
    for ref in refs[:-1]:
        total = total + ref[...].astype(jnp.float32)
    refs[-1][...] = total.astype(refs[-1].dtype)


def call(kernel, outs, args, flops=0, scalars=0, scratch=()):
    outs = [jax.ShapeDtypeStruct(shape, dtype) for shape, dtype in outs]
    vmem = pl.BlockSpec(memory_space=pltpu.VMEM)
    smem = pl.BlockSpec(memory_space=pltpu.SMEM)
    moved = sum(a.size * a.dtype.itemsize for a in [*args, *outs])
    results = pl.pallas_call(
        kernel,
        out_shape=outs,
        in_specs=[smem] * scalars + [vmem] * (len(args) - scalars),
        out_specs=[vmem] * len(outs),
        scratch_shapes=scratch,
        cost_estimate=pl.CostEstimate(flops=flops, bytes_accessed=moved, transcendentals=0),
        compiler_params=pltpu.CompilerParams(vmem_limit_bytes=24 << 20),
    )(*args)
    return results[0] if len(outs) == 1 else results


def shards(enc_out, kv_weight, queries, out_grad):
    rows, model = enc_out.shape
    depth, both = kv_weight.shape[1:]
    sections = lax.axis_size("section")
    width = Z_HI * depth
    low, high = jnp.bfloat16, jnp.float32
    near_groups = [[far * NEAR + near for near in range(NEAR)] for far in range(Z_HI)]
    far_groups = [[far * NEAR + near for far in range(Z_HI)] for near in range(NEAR)]
    place = lax.div(lax.axis_index("dp"), NEAR).astype(jnp.int32).reshape(1)
    work = 2 * NEAR * rows * width * both

    def shifted(array, step):
        pairs = [
            (far * NEAR + near, (far + step) % Z_HI * NEAR + near) for far in range(Z_HI) for near in range(NEAR)
        ]
        return lax.ppermute(array, "dp", pairs)

    def exchange(array, axis, groups=None):
        return lax.all_to_all(array, axis, 0, 0, axis_index_groups=groups)

    enc = call(split_columns, [((NEAR, rows, width), low)], [enc_out])
    own, enc = lax.optimization_barrier((kv_weight[0], enc))
    enc = exchange(enc, "dp", near_groups)
    weights = lax.all_gather(own, "dp", axis=0, tiled=True, axis_index_groups=far_groups)
    kv = call(project, [((NEAR, rows, both), high)], [enc, weights], flops=work)
    kv = exchange(kv, "dp", near_groups)
    dkv = call(attend, [((rows, both), low)], [kv, queries[0], out_grad[0]], flops=8 * rows * queries.size)
    dkv = exchange(jnp.broadcast_to(dkv[None], (NEAR, rows, both)), "dp", near_groups)
    line = sections // Z_LO
    line_groups = [[up * line + step for step in range(line)] for up in range(Z_LO)]
    piece = NEAR * rows // line

    def lowered(array, step):
        pairs = [(up * line + at, (up - step) * line + at) for up in range(step, Z_LO) for at in range(line)]
        return lax.ppermute(array, "section", pairs)

    part = call(spread, [((line, piece, width), low)], [dkv, weights], flops=work)
    part, dkv = lax.optimization_barrier((part, dkv))
    part = exchange(part, "section", line_groups)
    mine, after, beyond, before = call(
        weight_terms,
        [((depth, both), high)] * 2 + [((depth, both), low)] * 2,
        [place, enc, dkv],
        flops=work,
        scalars=1,
        scratch=[pltpu.VMEM((Z_HI, depth, both), high)],
    )
    beyond = shifted(beyond, 1)
    before = shifted(before, 3)
    total = call(row_total, [((piece, width), low)], [part])
    above = [lowered(total, step) for step in range(1, Z_LO)]
    above, beyond = lax.optimization_barrier((above, beyond))
    sums = call(suffix_sums, [((line, piece, width), low)], [part, *above])
    sums = exchange(sums, "section", line_groups)
    sums = exchange(sums.reshape(NEAR, rows, width), "dp", near_groups)
    after = call(add_terms, [((depth, both), low)], [after, beyond])
    after = shifted(after, 1)
    mine = call(add_terms, [((depth, both), high)], [mine, before], flops=30_000_000_000)
    sums, mine = lax.optimization_barrier((sums, mine))
    enc_grad = call(join_columns, [((1, rows, model), low)], [sums])
    enc_grad, mine, after = lax.optimization_barrier((enc_grad, mine, after))
    weight_grad = call(add_terms, [((depth, both), high)], [mine, after])[None]
    return enc_grad, weight_grad


def solution(mesh):
    in_specs = (
        P("dp", None),
        P("section", "dp", None),
        P("section", "dp", None),
        P("section", "dp", None),
    )
    out_specs = (P("section", "dp", None), P("section", "dp", None))
    return jax.shard_map(shards, mesh=mesh, in_specs=in_specs, out_specs=out_specs, check_vma=False)
```

```python
import jax
import jax.numpy as jnp
from jax import lax
from jax.experimental import pallas as pl
from jax.experimental.pallas import tpu as pltpu
from jax.sharding import PartitionSpec as P

Z_HI = 4
Z_LO = 4
NEAR = 8


def contract(left, right, left_dim, right_dim):
    return lax.dot_general(
        left, right, (((left_dim,), (right_dim,)), ((), ())), preferred_element_type=jnp.float32
    )


def split_columns(enc_ref, out_ref):
    width = out_ref.shape[2] // Z_HI
    for near in range(NEAR):
        for far in range(Z_HI):
            start = (far * NEAR + near) * width
            out_ref[near, :, far * width : (far + 1) * width] = enc_ref[:, start : start + width]


def join_columns(in_ref, out_ref):
    line = in_ref.shape[0] // NEAR
    part = in_ref.shape[1] // 2
    width = 2 * in_ref.shape[2] // Z_HI
    for near in range(NEAR):
        blocks = [in_ref[at * NEAR + near].astype(jnp.float32) for at in range(line)]
        blocks = [jnp.concatenate([block[:part], block[part:]], axis=1) for block in blocks]
        block = jnp.concatenate(blocks, axis=0).astype(jnp.bfloat16)
        for far in range(Z_HI):
            start = (far * NEAR + near) * width
            out_ref[0, :, start : start + width] = block[:, far * width : (far + 1) * width]


def project(enc_ref, weights_ref, kv_ref):
    near, rows, width = enc_ref.shape
    enc = enc_ref[...].reshape(near * rows, width)
    kv = jnp.dot(enc, weights_ref[...], preferred_element_type=jnp.float32)
    kv_ref[...] = kv.reshape(near, rows, kv.shape[1])


def attend(kv_ref, queries_ref, grad_ref, dkv_ref):
    kv = kv_ref[0]
    for near in range(1, kv_ref.shape[0]):
        kv = kv + kv_ref[near]
    kv = kv.astype(jnp.bfloat16)
    head = queries_ref.shape[1]
    scale = 1.0 / head**0.5
    queries = queries_ref[...]
    grad = grad_ref[...]
    scores = contract(kv[:, :head], queries, 1, 1) * scale
    expd = jnp.exp(scores - jnp.max(scores, axis=0, keepdims=True))
    probs = expd / jnp.sum(expd, axis=0, keepdims=True)
    dprobs = contract(kv[:, head:], grad, 1, 1)
    delta = jnp.sum(probs * dprobs, axis=0, keepdims=True)
    dscores = (probs * (dprobs - delta) * scale).astype(jnp.bfloat16)
    dkv_ref[:, :head] = contract(dscores, queries, 1, 0).astype(jnp.bfloat16)
    dkv_ref[:, head:] = contract(probs.astype(jnp.bfloat16), grad, 1, 0).astype(jnp.bfloat16)


def spread(dkv_ref, weights_ref, out_ref):
    line, piece, width = out_ref.shape
    near, rows, both = dkv_ref.shape
    part = rows // line
    dkv = dkv_ref[...].astype(jnp.float32)
    dkv = [dkv[:, at * part : (at + 1) * part].reshape(piece, both) for at in range(line)]
    dkv = jnp.concatenate(dkv, axis=0).astype(jnp.bfloat16)
    out = contract(dkv, weights_ref[...], 1, 1)
    out_ref[...] = out.astype(jnp.bfloat16).reshape(out_ref.shape)


def weight_terms(place_ref, enc_ref, dkv_ref, own_ref, next_ref, far_ref, last_ref, terms_ref):
    near, rows, width = dkv_ref.shape
    dkv = dkv_ref[...].reshape(near * rows, width)
    enc = enc_ref[...].reshape(near * rows, enc_ref.shape[2])
    terms = contract(enc, dkv, 0, 0)
    depth = own_ref.shape[0]
    for far in range(Z_HI):
        terms_ref[far] = terms[far * depth : (far + 1) * depth]
    for step, ref in enumerate((own_ref, next_ref, far_ref, last_ref)):
        ref[...] = terms_ref[lax.rem(place_ref[0] + step, Z_HI)].astype(ref.dtype)


def row_total(in_ref, out_ref):
    total = in_ref[0].astype(jnp.float32)
    for step in range(1, in_ref.shape[0]):
        total = total + in_ref[step].astype(jnp.float32)
    out_ref[...] = total.astype(jnp.bfloat16)


def suffix_sums(in_ref, one_ref, two_ref, three_ref, out_ref):
    line, piece, width = in_ref.shape
    part = piece // NEAR
    half = width // 2
    total = one_ref[...].astype(jnp.float32) + two_ref[...].astype(jnp.float32) + three_ref[...].astype(jnp.float32)
    for at in range(line - 1, -1, -1):
        total = total + in_ref[at].astype(jnp.float32)
        left = total[:, :half].reshape(NEAR, part, half)
        right = total[:, half:].reshape(NEAR, part, half)
        out_ref[at * NEAR : (at + 1) * NEAR] = jnp.concatenate([left, right], axis=1).astype(jnp.bfloat16)


def add_terms(own_ref, *refs):
    total = own_ref[...]
    for ref in refs[:-1]:
        total = total + ref[...].astype(jnp.float32)
    refs[-1][...] = total.astype(refs[-1].dtype)


def call(kernel, outs, args, flops=0, scalars=0, scratch=()):
    outs = [jax.ShapeDtypeStruct(shape, dtype) for shape, dtype in outs]
    vmem = pl.BlockSpec(memory_space=pltpu.VMEM)
    smem = pl.BlockSpec(memory_space=pltpu.SMEM)
    moved = sum(a.size * a.dtype.itemsize for a in [*args, *outs])
    results = pl.pallas_call(
        kernel,
        out_shape=outs,
        in_specs=[smem] * scalars + [vmem] * (len(args) - scalars),
        out_specs=[vmem] * len(outs),
        scratch_shapes=scratch,
        cost_estimate=pl.CostEstimate(flops=flops, bytes_accessed=moved, transcendentals=0),
        compiler_params=pltpu.CompilerParams(vmem_limit_bytes=24 << 20),
    )(*args)
    return results[0] if len(outs) == 1 else results


def shards(enc_out, kv_weight, queries, out_grad):
    rows, model = enc_out.shape
    depth, both = kv_weight.shape[1:]
    sections = lax.axis_size("section")
    width = Z_HI * depth
    low, high = jnp.bfloat16, jnp.float32
    near_groups = [[far * NEAR + near for near in range(NEAR)] for far in range(Z_HI)]
    far_groups = [[far * NEAR + near for far in range(Z_HI)] for near in range(NEAR)]
    place = lax.div(lax.axis_index("dp"), NEAR).astype(jnp.int32).reshape(1)
    work = 2 * NEAR * rows * width * both

    def shifted(array, step):
        pairs = [
            (far * NEAR + near, (far + step) % Z_HI * NEAR + near) for far in range(Z_HI) for near in range(NEAR)
        ]
        return lax.ppermute(array, "dp", pairs)

    def exchange(array, axis, groups=None):
        return lax.all_to_all(array, axis, 0, 0, axis_index_groups=groups)

    enc = call(split_columns, [((NEAR, rows, width), low)], [enc_out])
    own, enc = lax.optimization_barrier((kv_weight[0], enc))
    enc = exchange(enc, "dp", near_groups)
    weights = lax.all_gather(own, "dp", axis=0, tiled=True, axis_index_groups=far_groups)
    kv = call(project, [((NEAR, rows, both), high)], [enc, weights], flops=work)
    kv = exchange(kv, "dp", near_groups)
    dkv = call(attend, [((rows, both), low)], [kv, queries[0], out_grad[0]], flops=8 * rows * queries.size)
    dkv = exchange(jnp.broadcast_to(dkv[None], (NEAR, rows, both)), "dp", near_groups)
    line = sections // Z_LO
    line_groups = [[up * line + step for step in range(line)] for up in range(Z_LO)]
    piece = NEAR * rows // line
    plane_groups = [
        [((up * line + at) * Z_HI + far) * NEAR + near for at in range(line) for near in range(NEAR)]
        for up in range(Z_LO)
        for far in range(Z_HI)
    ]

    def lowered(array, step):
        pairs = [(up * line + at, (up - step) * line + at) for up in range(step, Z_LO) for at in range(line)]
        return lax.ppermute(array, "section", pairs)

    part = call(spread, [((line, piece, width), low)], [dkv, weights], flops=work)
    part, dkv = lax.optimization_barrier((part, dkv))
    part = exchange(part, "section", line_groups)
    mine, after, beyond, before = call(
        weight_terms,
        [((depth, both), high)] * 2 + [((depth, both), low)] * 2,
        [place, enc, dkv],
        flops=work,
        scalars=1,
        scratch=[pltpu.VMEM((Z_HI, depth, both), high)],
    )
    beyond = shifted(beyond, 1)
    before = shifted(before, 3)
    total = call(row_total, [((piece, width), low)], [part])
    above = [lowered(total, step) for step in range(1, Z_LO)]
    above, beyond = lax.optimization_barrier((above, beyond))
    sums = call(suffix_sums, [((line * NEAR, 2 * piece // NEAR, width // 2), low)], [part, *above])
    sums = exchange(sums, ("section", "dp"), plane_groups)
    after = call(add_terms, [((depth, both), low)], [after, beyond])
    after = shifted(after, 1)
    enc_grad = call(join_columns, [((1, rows, model), low)], [sums])
    enc_grad, mine, after, before = lax.optimization_barrier((enc_grad, mine, after, before))
    weight_grad = call(add_terms, [((depth, both), high)], [mine, after, before])[None]
    return enc_grad, weight_grad


def solution(mesh):
    in_specs = (
        P("dp", None),
        P("section", "dp", None),
        P("section", "dp", None),
        P("section", "dp", None),
    )
    out_specs = (P("section", "dp", None), P("section", "dp", None))
    return jax.shard_map(shards, mesh=mesh, in_specs=in_specs, out_specs=out_specs, check_vma=False)
```

```python
import jax
import jax.numpy as jnp
from jax import lax
from jax.experimental import pallas as pl
from jax.experimental.pallas import tpu as pltpu
from jax.sharding import PartitionSpec as P

Z_HI = 4
Z_LO = 4
NEAR = 8


def contract(left, right, left_dim, right_dim):
    return lax.dot_general(
        left, right, (((left_dim,), (right_dim,)), ((), ())), preferred_element_type=jnp.float32
    )


def split_columns(enc_ref, out_ref):
    width = out_ref.shape[2] // Z_HI
    for near in range(NEAR):
        for far in range(Z_HI):
            start = (far * NEAR + near) * width
            out_ref[near, :, far * width : (far + 1) * width] = enc_ref[:, start : start + width]


def join_columns(in_ref, out_ref):
    line = in_ref.shape[0] // NEAR
    part = in_ref.shape[1] // 2
    width = 2 * in_ref.shape[2] // Z_HI
    for near in range(NEAR):
        blocks = [in_ref[at * NEAR + near].astype(jnp.float32) for at in range(line)]
        blocks = [jnp.concatenate([block[:part], block[part:]], axis=1) for block in blocks]
        block = jnp.concatenate(blocks, axis=0).astype(jnp.bfloat16)
        for far in range(Z_HI):
            start = (far * NEAR + near) * width
            out_ref[0, :, start : start + width] = block[:, far * width : (far + 1) * width]


def project(enc_ref, weights_ref, kv_ref):
    near, rows, width = enc_ref.shape
    enc = enc_ref[...].reshape(near * rows, width)
    kv = jnp.dot(enc, weights_ref[...], preferred_element_type=jnp.float32)
    kv_ref[...] = kv.reshape(near, rows, kv.shape[1])


def attend(kv_ref, queries_ref, grad_ref, dkv_ref):
    kv = kv_ref[0]
    for near in range(1, kv_ref.shape[0]):
        kv = kv + kv_ref[near]
    kv = kv.astype(jnp.bfloat16)
    head = queries_ref.shape[1]
    scale = 1.0 / head**0.5
    queries = queries_ref[...]
    grad = grad_ref[...]
    scores = contract(kv[:, :head], queries, 1, 1) * scale
    expd = jnp.exp(scores - jnp.max(scores, axis=0, keepdims=True))
    probs = expd / jnp.sum(expd, axis=0, keepdims=True)
    dprobs = contract(kv[:, head:], grad, 1, 1)
    delta = jnp.sum(probs * dprobs, axis=0, keepdims=True)
    dscores = (probs * (dprobs - delta) * scale).astype(jnp.bfloat16)
    dkv_ref[:, :head] = contract(dscores, queries, 1, 0).astype(jnp.bfloat16)
    dkv_ref[:, head:] = contract(probs.astype(jnp.bfloat16), grad, 1, 0).astype(jnp.bfloat16)


def spread(dkv_ref, weights_ref, out_ref):
    line, piece, width = out_ref.shape
    near, rows, both = dkv_ref.shape
    part = rows // line
    dkv = dkv_ref[...].astype(jnp.float32)
    dkv = [dkv[:, at * part : (at + 1) * part].reshape(piece, both) for at in range(line)]
    dkv = jnp.concatenate(dkv, axis=0).astype(jnp.bfloat16)
    out = contract(dkv, weights_ref[...], 1, 1)
    out_ref[...] = out.astype(jnp.bfloat16).reshape(out_ref.shape)


def weight_terms(place_ref, enc_ref, dkv_ref, own_ref, next_ref, far_ref, last_ref, terms_ref):
    near, rows, width = dkv_ref.shape
    dkv = dkv_ref[...].reshape(near * rows, width)
    enc = enc_ref[...].reshape(near * rows, enc_ref.shape[2])
    terms = contract(enc, dkv, 0, 0)
    depth = own_ref.shape[0]
    for far in range(Z_HI):
        terms_ref[far] = terms[far * depth : (far + 1) * depth]
    for step, ref in enumerate((own_ref, next_ref, far_ref, last_ref)):
        ref[...] = terms_ref[lax.rem(place_ref[0] + step, Z_HI)].astype(ref.dtype)


def row_total(in_ref, out_ref):
    total = in_ref[0].astype(jnp.float32)
    for step in range(1, in_ref.shape[0]):
        total = total + in_ref[step].astype(jnp.float32)
    out_ref[...] = total.astype(jnp.bfloat16)


def suffix_sums(in_ref, one_ref, two_ref, three_ref, out_ref):
    line, piece, width = in_ref.shape
    part = piece // NEAR
    half = width // 2
    total = one_ref[...].astype(jnp.float32) + two_ref[...].astype(jnp.float32) + three_ref[...].astype(jnp.float32)
    for at in range(line - 1, -1, -1):
        total = total + in_ref[at].astype(jnp.float32)
        left = total[:, :half].reshape(NEAR, part, half)
        right = total[:, half:].reshape(NEAR, part, half)
        out_ref[at * NEAR : (at + 1) * NEAR] = jnp.concatenate([left, right], axis=1).astype(jnp.bfloat16)


def add_terms(own_ref, *refs):
    total = own_ref[...]
    for ref in refs[:-1]:
        total = total + ref[...].astype(jnp.float32)
    refs[-1][...] = total.astype(refs[-1].dtype)


def call(kernel, outs, args, flops=0, scalars=0, scratch=()):
    outs = [jax.ShapeDtypeStruct(shape, dtype) for shape, dtype in outs]
    vmem = pl.BlockSpec(memory_space=pltpu.VMEM)
    smem = pl.BlockSpec(memory_space=pltpu.SMEM)
    moved = sum(a.size * a.dtype.itemsize for a in [*args, *outs])
    results = pl.pallas_call(
        kernel,
        out_shape=outs,
        in_specs=[smem] * scalars + [vmem] * (len(args) - scalars),
        out_specs=[vmem] * len(outs),
        scratch_shapes=scratch,
        cost_estimate=pl.CostEstimate(flops=flops, bytes_accessed=moved, transcendentals=0),
        compiler_params=pltpu.CompilerParams(vmem_limit_bytes=24 << 20),
    )(*args)
    return results[0] if len(outs) == 1 else results


def shards(enc_out, kv_weight, queries, out_grad):
    rows, model = enc_out.shape
    depth, both = kv_weight.shape[1:]
    sections = lax.axis_size("section")
    width = Z_HI * depth
    low, high = jnp.bfloat16, jnp.float32
    near_groups = [[far * NEAR + near for near in range(NEAR)] for far in range(Z_HI)]
    far_groups = [[far * NEAR + near for far in range(Z_HI)] for near in range(NEAR)]
    place = lax.div(lax.axis_index("dp"), NEAR).astype(jnp.int32).reshape(1)
    work = 2 * NEAR * rows * width * both

    def shifted(array, step):
        pairs = [
            (far * NEAR + near, (far + step) % Z_HI * NEAR + near) for far in range(Z_HI) for near in range(NEAR)
        ]
        return lax.ppermute(array, "dp", pairs)

    def exchange(array, axis, groups=None):
        return lax.all_to_all(array, axis, 0, 0, axis_index_groups=groups)

    enc = call(split_columns, [((NEAR, rows, width), low)], [enc_out])
    own, enc = lax.optimization_barrier((kv_weight[0], enc))
    enc = exchange(enc, "dp", near_groups)
    weights = lax.all_gather(own, "dp", axis=0, tiled=True, axis_index_groups=far_groups)
    kv = call(project, [((NEAR, rows, both), high)], [enc, weights], flops=work)
    kv = exchange(kv, "dp", near_groups)
    dkv = call(attend, [((rows, both), low)], [kv, queries[0], out_grad[0]], flops=8 * rows * queries.size)
    dkv = exchange(jnp.broadcast_to(dkv[None], (NEAR, rows, both)), "dp", near_groups)
    line = sections // Z_LO
    line_groups = [[up * line + step for step in range(line)] for up in range(Z_LO)]
    piece = NEAR * rows // line
    plane_groups = [
        [((up * line + at) * Z_HI + far) * NEAR + near for at in range(line) for near in range(NEAR)]
        for up in range(Z_LO)
        for far in range(Z_HI)
    ]

    def lowered(array, step):
        pairs = [(up * line + at, (up - step) * line + at) for up in range(step, Z_LO) for at in range(line)]
        return lax.ppermute(array, "section", pairs)

    part = call(spread, [((line, piece, width), low)], [dkv, weights], flops=work)
    part, dkv = lax.optimization_barrier((part, dkv))
    part = exchange(part, "section", line_groups)
    mine, after, beyond, before = call(
        weight_terms,
        [((depth, both), high)] * 2 + [((depth, both), low)] * 2,
        [place, enc, dkv],
        flops=work,
        scalars=1,
        scratch=[pltpu.VMEM((Z_HI, depth, both), high)],
    )
    beyond = shifted(beyond, 1)
    after = shifted(call(add_terms, [((depth, both), low)], [after, beyond]), 1)
    before = shifted(before, 3)
    total = call(row_total, [((piece, width), low)], [part])
    above = [lowered(total, step) for step in range(1, Z_LO)]
    above, beyond = lax.optimization_barrier((above, beyond))
    sums = call(suffix_sums, [((line * NEAR, 2 * piece // NEAR, width // 2), low)], [part, *above])
    sums = exchange(sums, ("section", "dp"), plane_groups)
    mine = call(add_terms, [((depth, both), high)], [mine, after], flops=int(8e9))
    mine = call(add_terms, [((depth, both), high)], [mine, before], flops=int(1e9))
    sums, mine = lax.optimization_barrier((sums, mine))
    enc_grad = call(join_columns, [((1, rows, model), low)], [sums])
    weight_grad = mine[None]
    return enc_grad, weight_grad


def solution(mesh):
    in_specs = (
        P("dp", None),
        P("section", "dp", None),
        P("section", "dp", None),
        P("section", "dp", None),
    )
    out_specs = (P("section", "dp", None), P("section", "dp", None))
    return jax.shard_map(shards, mesh=mesh, in_specs=in_specs, out_specs=out_specs, check_vma=False)
```

```python
import jax
import jax.numpy as jnp
from jax import lax
from jax.experimental import pallas as pl
from jax.experimental.pallas import tpu as pltpu
from jax.sharding import PartitionSpec as P

Z_HI = 4
Z_LO = 4
NEAR = 8


def contract(left, right, left_dim, right_dim):
    return lax.dot_general(
        left, right, (((left_dim,), (right_dim,)), ((), ())), preferred_element_type=jnp.float32
    )


def split_columns(enc_ref, out_ref):
    width = out_ref.shape[2] // Z_HI
    for near in range(NEAR):
        for far in range(Z_HI):
            start = (far * NEAR + near) * width
            out_ref[near, :, far * width : (far + 1) * width] = enc_ref[:, start : start + width]


def join_columns(in_ref, out_ref):
    line = in_ref.shape[0] // NEAR
    part = in_ref.shape[1] // 2
    width = 2 * in_ref.shape[2] // Z_HI
    for near in range(NEAR):
        blocks = [in_ref[at * NEAR + near].astype(jnp.float32) for at in range(line)]
        blocks = [jnp.concatenate([block[:part], block[part:]], axis=1) for block in blocks]
        block = jnp.concatenate(blocks, axis=0).astype(jnp.bfloat16)
        for far in range(Z_HI):
            start = (far * NEAR + near) * width
            out_ref[0, :, start : start + width] = block[:, far * width : (far + 1) * width]


def project(enc_ref, weights_ref, kv_ref):
    near, rows, width = enc_ref.shape
    enc = enc_ref[...].reshape(near * rows, width)
    kv = jnp.dot(enc, weights_ref[...], preferred_element_type=jnp.float32)
    kv_ref[...] = kv.reshape(near, rows, kv.shape[1])


def attend(kv_ref, queries_ref, grad_ref, dkv_ref):
    kv = kv_ref[0]
    for near in range(1, kv_ref.shape[0]):
        kv = kv + kv_ref[near]
    kv = kv.astype(jnp.bfloat16)
    head = queries_ref.shape[1]
    scale = 1.0 / head**0.5
    queries = queries_ref[...]
    grad = grad_ref[...]
    scores = contract(kv[:, :head], queries, 1, 1) * scale
    expd = jnp.exp(scores - jnp.max(scores, axis=0, keepdims=True))
    probs = expd / jnp.sum(expd, axis=0, keepdims=True)
    dprobs = contract(kv[:, head:], grad, 1, 1)
    delta = jnp.sum(probs * dprobs, axis=0, keepdims=True)
    dscores = (probs * (dprobs - delta) * scale).astype(jnp.bfloat16)
    dkv_ref[:, :head] = contract(dscores, queries, 1, 0).astype(jnp.bfloat16)
    dkv_ref[:, head:] = contract(probs.astype(jnp.bfloat16), grad, 1, 0).astype(jnp.bfloat16)


def spread(dkv_ref, weights_ref, out_ref):
    line, piece, width = out_ref.shape
    near, rows, both = dkv_ref.shape
    part = rows // line
    dkv = dkv_ref[...].astype(jnp.float32)
    dkv = [dkv[:, at * part : (at + 1) * part].reshape(piece, both) for at in range(line)]
    dkv = jnp.concatenate(dkv, axis=0).astype(jnp.bfloat16)
    out = contract(dkv, weights_ref[...], 1, 1)
    out_ref[...] = out.astype(jnp.bfloat16).reshape(out_ref.shape)


def weight_terms(place_ref, enc_ref, dkv_ref, own_ref, next_ref, far_ref, last_ref, terms_ref):
    near, rows, width = dkv_ref.shape
    dkv = dkv_ref[...].reshape(near * rows, width)
    enc = enc_ref[...].reshape(near * rows, enc_ref.shape[2])
    terms = contract(enc, dkv, 0, 0)
    depth = own_ref.shape[0]
    for far in range(Z_HI):
        terms_ref[far] = terms[far * depth : (far + 1) * depth]
    for step, ref in enumerate((own_ref, next_ref, far_ref, last_ref)):
        ref[...] = terms_ref[lax.rem(place_ref[0] + step, Z_HI)].astype(ref.dtype)


def row_total(in_ref, out_ref):
    total = in_ref[0].astype(jnp.float32)
    for step in range(1, in_ref.shape[0]):
        total = total + in_ref[step].astype(jnp.float32)
    out_ref[...] = total.astype(jnp.bfloat16)


def suffix_sums(in_ref, one_ref, two_ref, three_ref, out_ref):
    line, piece, width = in_ref.shape
    part = piece // NEAR
    half = width // 2
    total = one_ref[...].astype(jnp.float32) + two_ref[...].astype(jnp.float32) + three_ref[...].astype(jnp.float32)
    for at in range(line - 1, -1, -1):
        total = total + in_ref[at].astype(jnp.float32)
        left = total[:, :half].reshape(NEAR, part, half)
        right = total[:, half:].reshape(NEAR, part, half)
        out_ref[at * NEAR : (at + 1) * NEAR] = jnp.concatenate([left, right], axis=1).astype(jnp.bfloat16)


def add_terms(own_ref, *refs):
    total = own_ref[...]
    for ref in refs[:-1]:
        total = total + ref[...].astype(jnp.float32)
    refs[-1][...] = total.astype(refs[-1].dtype)


def call(kernel, outs, args, flops=0, scalars=0, scratch=()):
    outs = [jax.ShapeDtypeStruct(shape, dtype) for shape, dtype in outs]
    vmem = pl.BlockSpec(memory_space=pltpu.VMEM)
    smem = pl.BlockSpec(memory_space=pltpu.SMEM)
    moved = sum(a.size * a.dtype.itemsize for a in [*args, *outs])
    results = pl.pallas_call(
        kernel,
        out_shape=outs,
        in_specs=[smem] * scalars + [vmem] * (len(args) - scalars),
        out_specs=[vmem] * len(outs),
        scratch_shapes=scratch,
        cost_estimate=pl.CostEstimate(flops=flops, bytes_accessed=moved, transcendentals=0),
        compiler_params=pltpu.CompilerParams(vmem_limit_bytes=24 << 20),
    )(*args)
    return results[0] if len(outs) == 1 else results


def shards(enc_out, kv_weight, queries, out_grad):
    rows, model = enc_out.shape
    depth, both = kv_weight.shape[1:]
    sections = lax.axis_size("section")
    line = sections // Z_LO
    width = Z_HI * depth
    low, high = jnp.bfloat16, jnp.float32
    near_groups = [[far * NEAR + near for near in range(NEAR)] for far in range(Z_HI)]
    far_groups = [[far * NEAR + near for far in range(Z_HI)] for near in range(NEAR)]
    place = lax.div(lax.axis_index("dp"), NEAR).astype(jnp.int32).reshape(1)
    work = 2 * NEAR * rows * width * both

    def shifted(array, step):
        pairs = [
            (far * NEAR + near, (far + step) % Z_HI * NEAR + near) for far in range(Z_HI) for near in range(NEAR)
        ]
        return lax.ppermute(array, "dp", pairs)

    def returned(array, ups):
        pairs = [
            ((up * line + at) * Z_HI * NEAR + far * NEAR + near, (up * line + at) * Z_HI * NEAR + (far - 1) % Z_HI * NEAR + near)
            for up in ups
            for at in range(line)
            for far in range(Z_HI)
            for near in range(NEAR)
        ]
        return lax.ppermute(array, ("section", "dp"), pairs)

    def exchange(array, axis, groups=None):
        return lax.all_to_all(array, axis, 0, 0, axis_index_groups=groups)

    enc = call(split_columns, [((NEAR, rows, width), low)], [enc_out])
    own, enc = lax.optimization_barrier((kv_weight[0], enc))
    enc = exchange(enc, "dp", near_groups)
    weights = lax.all_gather(own, "dp", axis=0, tiled=True, axis_index_groups=far_groups)
    kv = call(project, [((NEAR, rows, both), high)], [enc, weights], flops=work)
    kv = exchange(kv, "dp", near_groups)
    dkv = call(attend, [((rows, both), low)], [kv, queries[0], out_grad[0]], flops=8 * rows * queries.size)
    dkv = exchange(jnp.broadcast_to(dkv[None], (NEAR, rows, both)), "dp", near_groups)
    line_groups = [[up * line + step for step in range(line)] for up in range(Z_LO)]
    piece = NEAR * rows // line
    plane_groups = [
        [((up * line + at) * Z_HI + far) * NEAR + near for at in range(line) for near in range(NEAR)]
        for up in range(Z_LO)
        for far in range(Z_HI)
    ]

    def lowered(array, step):
        pairs = [(up * line + at, (up - step) * line + at) for up in range(step, Z_LO) for at in range(line)]
        return lax.ppermute(array, "section", pairs)

    part = call(spread, [((line, piece, width), low)], [dkv, weights], flops=work)
    part, dkv = lax.optimization_barrier((part, dkv))
    part = exchange(part, "section", line_groups)
    mine, after, beyond, before = call(
        weight_terms,
        [((depth, both), high)] * 2 + [((depth, both), low)] * 2,
        [place, enc, dkv],
        flops=work,
        scalars=1,
        scratch=[pltpu.VMEM((Z_HI, depth, both), high)],
    )
    beyond = shifted(beyond, 1)
    after = shifted(call(add_terms, [((depth, both), low)], [after, beyond]), 1)
    lower, upper = returned(before, range(Z_LO // 2)), returned(before, range(Z_LO // 2, Z_LO))
    total = call(row_total, [((piece, width), low)], [part])
    above = [lowered(total, step) for step in range(Z_LO - 1, 0, -1)]
    above, beyond = lax.optimization_barrier((above, beyond))
    sums = call(suffix_sums, [((line * NEAR, 2 * piece // NEAR, width // 2), low)], [part, *above])
    sums = exchange(sums, ("section", "dp"), plane_groups)
    mine = call(add_terms, [((depth, both), high)], [mine, after, upper], flops=int(4e9))
    sums, mine = lax.optimization_barrier((sums, mine))
    enc_grad = call(join_columns, [((1, rows, model), low)], [sums])
    enc_grad, mine, lower = lax.optimization_barrier((enc_grad, mine, lower))
    weight_grad = call(add_terms, [((depth, both), high)], [mine, lower])[None]
    return enc_grad, weight_grad


def solution(mesh):
    in_specs = (
        P("dp", None),
        P("section", "dp", None),
        P("section", "dp", None),
        P("section", "dp", None),
    )
    out_specs = (P("section", "dp", None), P("section", "dp", None))
    return jax.shard_map(shards, mesh=mesh, in_specs=in_specs, out_specs=out_specs, check_vma=False)
```

```python
import jax
import jax.numpy as jnp
from jax import lax
from jax.experimental import pallas as pl
from jax.experimental.pallas import tpu as pltpu
from jax.sharding import PartitionSpec as P

Z_HI = 4
Z_LO = 4
NEAR = 8


def contract(left, right, left_dim, right_dim):
    return lax.dot_general(
        left, right, (((left_dim,), (right_dim,)), ((), ())), preferred_element_type=jnp.float32
    )


def split_columns(enc_ref, out_ref):
    width = out_ref.shape[2] // Z_HI
    for near in range(NEAR):
        for far in range(Z_HI):
            start = (far * NEAR + near) * width
            out_ref[near, :, far * width : (far + 1) * width] = enc_ref[:, start : start + width]


def join_columns(in_ref, out_ref):
    line = in_ref.shape[0] // NEAR
    part = in_ref.shape[1] // 2
    width = 2 * in_ref.shape[2] // Z_HI
    for near in range(NEAR):
        blocks = [in_ref[at * NEAR + near].astype(jnp.float32) for at in range(line)]
        blocks = [jnp.concatenate([block[:part], block[part:]], axis=1) for block in blocks]
        block = jnp.concatenate(blocks, axis=0).astype(jnp.bfloat16)
        for far in range(Z_HI):
            start = (far * NEAR + near) * width
            out_ref[0, :, start : start + width] = block[:, far * width : (far + 1) * width]


def project(enc_ref, weights_ref, kv_ref):
    near, rows, width = enc_ref.shape
    enc = enc_ref[...].reshape(near * rows, width)
    kv = jnp.dot(enc, weights_ref[...], preferred_element_type=jnp.float32)
    kv_ref[...] = kv.reshape(near, rows, kv.shape[1])


def attend(kv_ref, queries_ref, grad_ref, dkv_ref):
    kv = kv_ref[0]
    for near in range(1, kv_ref.shape[0]):
        kv = kv + kv_ref[near]
    kv = kv.astype(jnp.bfloat16)
    head = queries_ref.shape[1]
    scale = 1.0 / head**0.5
    queries = queries_ref[...]
    grad = grad_ref[...]
    scores = contract(kv[:, :head], queries, 1, 1) * scale
    expd = jnp.exp(scores - jnp.max(scores, axis=0, keepdims=True))
    probs = expd / jnp.sum(expd, axis=0, keepdims=True)
    dprobs = contract(kv[:, head:], grad, 1, 1)
    delta = jnp.sum(probs * dprobs, axis=0, keepdims=True)
    dscores = (probs * (dprobs - delta) * scale).astype(jnp.bfloat16)
    dkv_ref[:, :head] = contract(dscores, queries, 1, 0).astype(jnp.bfloat16)
    dkv_ref[:, head:] = contract(probs.astype(jnp.bfloat16), grad, 1, 0).astype(jnp.bfloat16)


def spread(dkv_ref, weights_ref, out_ref):
    line, piece, width = out_ref.shape
    near, rows, both = dkv_ref.shape
    part = rows // line
    dkv = dkv_ref[...].astype(jnp.float32)
    dkv = [dkv[:, at * part : (at + 1) * part].reshape(piece, both) for at in range(line)]
    dkv = jnp.concatenate(dkv, axis=0).astype(jnp.bfloat16)
    out = contract(dkv, weights_ref[...], 1, 1)
    out_ref[...] = out.astype(jnp.bfloat16).reshape(out_ref.shape)


def weight_terms(place_ref, enc_ref, dkv_ref, own_ref, next_ref, far_ref, last_ref, terms_ref):
    near, rows, width = dkv_ref.shape
    dkv = dkv_ref[...].reshape(near * rows, width)
    enc = enc_ref[...].reshape(near * rows, enc_ref.shape[2])
    terms = contract(enc, dkv, 0, 0)
    depth = own_ref.shape[0]
    for far in range(Z_HI):
        terms_ref[far] = terms[far * depth : (far + 1) * depth]
    for step, ref in enumerate((own_ref, next_ref, far_ref, last_ref)):
        ref[...] = terms_ref[lax.rem(place_ref[0] + step, Z_HI)].astype(ref.dtype)


def row_total(in_ref, out_ref):
    total = in_ref[0].astype(jnp.float32)
    for step in range(1, in_ref.shape[0]):
        total = total + in_ref[step].astype(jnp.float32)
    out_ref[...] = total.astype(jnp.bfloat16)


def suffix_sums(in_ref, one_ref, two_ref, three_ref, out_ref):
    line, piece, width = in_ref.shape
    part = piece // NEAR
    half = width // 2
    total = one_ref[...].astype(jnp.float32) + two_ref[...].astype(jnp.float32) + three_ref[...].astype(jnp.float32)
    for at in range(line - 1, -1, -1):
        total = total + in_ref[at].astype(jnp.float32)
        left = total[:, :half].reshape(NEAR, part, half)
        right = total[:, half:].reshape(NEAR, part, half)
        out_ref[at * NEAR : (at + 1) * NEAR] = jnp.concatenate([left, right], axis=1).astype(jnp.bfloat16)


def add_terms(own_ref, *refs):
    total = own_ref[...]
    for ref in refs[:-1]:
        total = total + ref[...].astype(jnp.float32)
    refs[-1][...] = total.astype(refs[-1].dtype)


def call(kernel, outs, args, flops=0, scalars=0, scratch=()):
    outs = [jax.ShapeDtypeStruct(shape, dtype) for shape, dtype in outs]
    vmem = pl.BlockSpec(memory_space=pltpu.VMEM)
    smem = pl.BlockSpec(memory_space=pltpu.SMEM)
    moved = sum(a.size * a.dtype.itemsize for a in [*args, *outs])
    results = pl.pallas_call(
        kernel,
        out_shape=outs,
        in_specs=[smem] * scalars + [vmem] * (len(args) - scalars),
        out_specs=[vmem] * len(outs),
        scratch_shapes=scratch,
        cost_estimate=pl.CostEstimate(flops=flops, bytes_accessed=moved, transcendentals=0),
        compiler_params=pltpu.CompilerParams(vmem_limit_bytes=24 << 20),
    )(*args)
    return results[0] if len(outs) == 1 else results


def shards(enc_out, kv_weight, queries, out_grad):
    rows, model = enc_out.shape
    depth, both = kv_weight.shape[1:]
    sections = lax.axis_size("section")
    line = sections // Z_LO
    width = Z_HI * depth
    low, high = jnp.bfloat16, jnp.float32
    near_groups = [[far * NEAR + near for near in range(NEAR)] for far in range(Z_HI)]
    far_groups = [[far * NEAR + near for far in range(Z_HI)] for near in range(NEAR)]
    place = lax.div(lax.axis_index("dp"), NEAR).astype(jnp.int32).reshape(1)
    work = 2 * NEAR * rows * width * both

    def shifted(array, step):
        pairs = [
            (far * NEAR + near, (far + step) % Z_HI * NEAR + near) for far in range(Z_HI) for near in range(NEAR)
        ]
        return lax.ppermute(array, "dp", pairs)

    def returned(array, ups):
        pairs = [
            ((up * line + at) * Z_HI * NEAR + far * NEAR + near, (up * line + at) * Z_HI * NEAR + (far - 1) % Z_HI * NEAR + near)
            for up in ups
            for at in range(line)
            for far in range(Z_HI)
            for near in range(NEAR)
        ]
        return lax.ppermute(array, ("section", "dp"), pairs)

    def exchange(array, axis, groups=None):
        return lax.all_to_all(array, axis, 0, 0, axis_index_groups=groups)

    enc = call(split_columns, [((NEAR, rows, width), low)], [enc_out])
    own, enc = lax.optimization_barrier((kv_weight[0], enc))
    enc = exchange(enc, "dp", near_groups)
    weights = lax.all_gather(own, "dp", axis=0, tiled=True, axis_index_groups=far_groups)
    kv = call(project, [((NEAR, rows, both), high)], [enc, weights], flops=work)
    kv = exchange(kv, "dp", near_groups)
    dkv = call(attend, [((rows, both), low)], [kv, queries[0], out_grad[0]], flops=8 * rows * queries.size)
    dkv = exchange(jnp.broadcast_to(dkv[None], (NEAR, rows, both)), "dp", near_groups)
    line_groups = [[up * line + step for step in range(line)] for up in range(Z_LO)]
    piece = NEAR * rows // line
    plane_groups = [
        [((up * line + at) * Z_HI + far) * NEAR + near for at in range(line) for near in range(NEAR)]
        for up in range(Z_LO)
        for far in range(Z_HI)
    ]

    def lowered(array, step):
        pairs = [(up * line + at, (up - step) * line + at) for up in range(step, Z_LO) for at in range(line)]
        return lax.ppermute(array, "section", pairs)

    part = call(spread, [((line, piece, width), low)], [dkv, weights], flops=work)
    part, dkv = lax.optimization_barrier((part, dkv))
    part = exchange(part, "section", line_groups)
    mine, after, beyond, before = call(
        weight_terms,
        [((depth, both), high)] * 2 + [((depth, both), low)] * 2,
        [place, enc, dkv],
        flops=work,
        scalars=1,
        scratch=[pltpu.VMEM((Z_HI, depth, both), high)],
    )
    beyond = shifted(beyond, 1)
    after = shifted(call(add_terms, [((depth, both), low)], [after, beyond]), 1)
    lower, upper = returned(before, range(Z_LO // 2)), returned(before, range(Z_LO // 2, Z_LO))
    total = call(row_total, [((piece, width), low)], [part])
    above = [lowered(total, step) for step in (2,3,1)]
    above, beyond = lax.optimization_barrier((above, beyond))
    sums = call(suffix_sums, [((line * NEAR, 2 * piece // NEAR, width // 2), low)], [part, *above])
    sums = exchange(sums, ("section", "dp"), plane_groups)
    mine = call(add_terms, [((depth, both), high)], [mine, after, upper], flops=int(4e9))
    sums, mine = lax.optimization_barrier((sums, mine))
    enc_grad = call(join_columns, [((1, rows, model), low)], [sums])
    enc_grad, mine, lower = lax.optimization_barrier((enc_grad, mine, lower))
    weight_grad = call(add_terms, [((depth, both), high)], [mine, lower])[None]
    return enc_grad, weight_grad


def solution(mesh):
    in_specs = (
        P("dp", None),
        P("section", "dp", None),
        P("section", "dp", None),
        P("section", "dp", None),
    )
    out_specs = (P("section", "dp", None), P("section", "dp", None))
    return jax.shard_map(shards, mesh=mesh, in_specs=in_specs, out_specs=out_specs, check_vma=False)
```

```python
import jax
import jax.numpy as jnp
from jax import lax
from jax.experimental import pallas as pl
from jax.experimental.pallas import tpu as pltpu
from jax.sharding import PartitionSpec as P

Z_HI = 4
Z_LO = 4
NEAR = 8


def contract(left, right, left_dim, right_dim):
    return lax.dot_general(
        left, right, (((left_dim,), (right_dim,)), ((), ())), preferred_element_type=jnp.float32
    )


def split_columns(enc_ref, out_ref):
    width = out_ref.shape[2] // Z_HI
    for near in range(NEAR):
        for far in range(Z_HI):
            start = (far * NEAR + near) * width
            out_ref[near, :, far * width : (far + 1) * width] = enc_ref[:, start : start + width]


def join_columns(in_ref, out_ref):
    line = in_ref.shape[0] // NEAR
    part = in_ref.shape[1] // 2
    width = 2 * in_ref.shape[2] // Z_HI
    for near in range(NEAR):
        blocks = [in_ref[at * NEAR + near].astype(jnp.float32) for at in range(line)]
        blocks = [jnp.concatenate([block[:part], block[part:]], axis=1) for block in blocks]
        block = jnp.concatenate(blocks, axis=0).astype(jnp.bfloat16)
        for far in range(Z_HI):
            start = (far * NEAR + near) * width
            out_ref[0, :, start : start + width] = block[:, far * width : (far + 1) * width]


def project(enc_ref, weights_ref, kv_ref):
    near, rows, width = enc_ref.shape
    enc = enc_ref[...].reshape(near * rows, width)
    kv = jnp.dot(enc, weights_ref[...], preferred_element_type=jnp.float32)
    kv_ref[...] = kv.reshape(near, rows, kv.shape[1])


def attend(kv_ref, queries_ref, grad_ref, dkv_ref):
    kv = kv_ref[0]
    for near in range(1, kv_ref.shape[0]):
        kv = kv + kv_ref[near]
    kv = kv.astype(jnp.bfloat16)
    head = queries_ref.shape[1]
    scale = 1.0 / head**0.5
    queries = queries_ref[...]
    grad = grad_ref[...]
    scores = contract(kv[:, :head], queries, 1, 1) * scale
    expd = jnp.exp(scores - jnp.max(scores, axis=0, keepdims=True))
    probs = expd / jnp.sum(expd, axis=0, keepdims=True)
    dprobs = contract(kv[:, head:], grad, 1, 1)
    delta = jnp.sum(probs * dprobs, axis=0, keepdims=True)
    dscores = (probs * (dprobs - delta) * scale).astype(jnp.bfloat16)
    dkv_ref[:, :head] = contract(dscores, queries, 1, 0).astype(jnp.bfloat16)
    dkv_ref[:, head:] = contract(probs.astype(jnp.bfloat16), grad, 1, 0).astype(jnp.bfloat16)


def spread(dkv_ref, weights_ref, out_ref):
    line, piece, width = out_ref.shape
    near, rows, both = dkv_ref.shape
    part = rows // line
    dkv = dkv_ref[...].astype(jnp.float32)
    dkv = [dkv[:, at * part : (at + 1) * part].reshape(piece, both) for at in range(line)]
    dkv = jnp.concatenate(dkv, axis=0).astype(jnp.bfloat16)
    out = contract(dkv, weights_ref[...], 1, 1)
    out_ref[...] = out.astype(jnp.bfloat16).reshape(out_ref.shape)


def weight_terms(place_ref, enc_ref, dkv_ref, own_ref, next_ref, far_ref, last_ref, terms_ref):
    near, rows, width = dkv_ref.shape
    dkv = dkv_ref[...].reshape(near * rows, width)
    enc = enc_ref[...].reshape(near * rows, enc_ref.shape[2])
    terms = contract(enc, dkv, 0, 0)
    depth = own_ref.shape[0]
    for far in range(Z_HI):
        terms_ref[far] = terms[far * depth : (far + 1) * depth]
    for step, ref in enumerate((own_ref, next_ref, far_ref, last_ref)):
        ref[...] = terms_ref[lax.rem(place_ref[0] + step, Z_HI)].astype(ref.dtype)


def row_total(in_ref, out_ref):
    total = in_ref[0].astype(jnp.float32)
    for step in range(1, in_ref.shape[0]):
        total = total + in_ref[step].astype(jnp.float32)
    out_ref[...] = total.astype(jnp.bfloat16)


def suffix_sums(in_ref, one_ref, two_ref, three_ref, out_ref):
    line, piece, width = in_ref.shape
    part = piece // NEAR
    half = width // 2
    total = one_ref[...].astype(jnp.float32) + two_ref[...].astype(jnp.float32) + three_ref[...].astype(jnp.float32)
    for at in range(line - 1, -1, -1):
        total = total + in_ref[at].astype(jnp.float32)
        left = total[:, :half].reshape(NEAR, part, half)
        right = total[:, half:].reshape(NEAR, part, half)
        out_ref[at * NEAR : (at + 1) * NEAR] = jnp.concatenate([left, right], axis=1).astype(jnp.bfloat16)


def add_terms(own_ref, *refs):
    total = own_ref[...]
    for ref in refs[:-1]:
        total = total + ref[...].astype(jnp.float32)
    refs[-1][...] = total.astype(refs[-1].dtype)


def finish(sums_ref, own_ref, lower_ref, last_ref, enc_grad_ref, weight_grad_ref):
    join_columns(sums_ref, enc_grad_ref)
    weight_grad_ref[0] = own_ref[...] + lower_ref[...].astype(jnp.float32) + last_ref[...].astype(jnp.float32)


def call(kernel, outs, args, flops=0, scalars=0, scratch=()):
    outs = [jax.ShapeDtypeStruct(shape, dtype) for shape, dtype in outs]
    vmem = pl.BlockSpec(memory_space=pltpu.VMEM)
    smem = pl.BlockSpec(memory_space=pltpu.SMEM)
    moved = sum(a.size * a.dtype.itemsize for a in [*args, *outs])
    results = pl.pallas_call(
        kernel,
        out_shape=outs,
        in_specs=[smem] * scalars + [vmem] * (len(args) - scalars),
        out_specs=[vmem] * len(outs),
        scratch_shapes=scratch,
        cost_estimate=pl.CostEstimate(flops=flops, bytes_accessed=moved, transcendentals=0),
        compiler_params=pltpu.CompilerParams(vmem_limit_bytes=24 << 20),
    )(*args)
    return results[0] if len(outs) == 1 else results


def shards(enc_out, kv_weight, queries, out_grad):
    rows, model = enc_out.shape
    depth, both = kv_weight.shape[1:]
    sections = lax.axis_size("section")
    line = sections // Z_LO
    width = Z_HI * depth
    low, high = jnp.bfloat16, jnp.float32
    near_groups = [[far * NEAR + near for near in range(NEAR)] for far in range(Z_HI)]
    far_groups = [[far * NEAR + near for far in range(Z_HI)] for near in range(NEAR)]
    place = lax.div(lax.axis_index("dp"), NEAR).astype(jnp.int32).reshape(1)
    work = 2 * NEAR * rows * width * both

    def shifted(array, step):
        pairs = [
            (far * NEAR + near, (far + step) % Z_HI * NEAR + near) for far in range(Z_HI) for near in range(NEAR)
        ]
        return lax.ppermute(array, "dp", pairs)

    def passed(array, way, chosen):
        pairs = [
            (
                ((up * line + at) * Z_HI + far) * NEAR + near,
                ((up * line + at) * Z_HI + (far + way) % Z_HI) * NEAR + near,
            )
            for up in range(Z_LO)
            for at in range(line)
            for far in range(Z_HI)
            for near in range(NEAR)
            if (up, near % 2) in chosen
        ]
        return lax.ppermute(array, ("section", "dp"), pairs)

    def exchange(array, axis, groups=None):
        return lax.all_to_all(array, axis, 0, 0, axis_index_groups=groups)

    enc = call(split_columns, [((NEAR, rows, width), low)], [enc_out])
    own, enc = lax.optimization_barrier((kv_weight[0], enc))
    enc = exchange(enc, "dp", near_groups)
    weights = lax.all_gather(own, "dp", axis=0, tiled=True, axis_index_groups=far_groups)
    kv = call(project, [((NEAR, rows, both), high)], [enc, weights], flops=work)
    kv = exchange(kv, "dp", near_groups)
    dkv = call(attend, [((rows, both), low)], [kv, queries[0], out_grad[0]], flops=8 * rows * queries.size)
    dkv = exchange(jnp.broadcast_to(dkv[None], (NEAR, rows, both)), "dp", near_groups)
    line_groups = [[up * line + step for step in range(line)] for up in range(Z_LO)]
    piece = NEAR * rows // line
    plane_groups = [
        [((up * line + at) * Z_HI + far) * NEAR + near for at in range(line) for near in range(NEAR)]
        for up in range(Z_LO)
        for far in range(Z_HI)
    ]

    def lowered(array, step):
        pairs = [(up * line + at, (up - step) * line + at) for up in range(step, Z_LO) for at in range(line)]
        return lax.ppermute(array, "section", pairs)

    part = call(spread, [((line, piece, width), low)], [dkv, weights], flops=work)
    part, dkv = lax.optimization_barrier((part, dkv))
    part = exchange(part, "section", line_groups)
    mine, after, beyond, before = call(
        weight_terms,
        [((depth, both), high)] * 2 + [((depth, both), low)] * 2,
        [place, enc, dkv],
        flops=work,
        scalars=1,
        scratch=[pltpu.VMEM((Z_HI, depth, both), high)],
    )
    beyond = shifted(beyond, 1)
    after = call(add_terms, [((depth, both), low)], [after, beyond])
    late = [(3, 0), (3, 1)]
    after, last = passed(after, 1, [(up, core) for up in range(3) for core in range(2)]), passed(after, 1, late)
    early = [(1, 1), (2, 0), (2, 1), (3, 0), (3, 1)]
    lower, upper = passed(before, -1, [(0, 0), (0, 1), (1, 0)]), passed(before, -1, early)
    total = call(row_total, [((piece, width), low)], [part])
    above = [lowered(total, step) for step in (3,2,1)]
    above, beyond = lax.optimization_barrier((above, beyond))
    sums = call(suffix_sums, [((line * NEAR, 2 * piece // NEAR, width // 2), low)], [part, *above])
    sums = exchange(sums, ("section", "dp"), plane_groups)
    mine = call(add_terms, [((depth, both), high)], [mine, after, upper], flops=int(4e9))
    sums, mine = lax.optimization_barrier((sums, mine))
    enc_grad, weight_grad = call(
        finish, [((1, rows, model), low), ((1, depth, both), high)], [sums, mine, lower, last]
    )
    return enc_grad, weight_grad


def solution(mesh):
    in_specs = (
        P("dp", None),
        P("section", "dp", None),
        P("section", "dp", None),
        P("section", "dp", None),
    )
    out_specs = (P("section", "dp", None), P("section", "dp", None))
    return jax.shard_map(shards, mesh=mesh, in_specs=in_specs, out_specs=out_specs, check_vma=False)
```

```python
import jax
import jax.numpy as jnp
from jax import lax
from jax.experimental import pallas as pl
from jax.experimental.pallas import tpu as pltpu
from jax.sharding import PartitionSpec as P

Z_HI = 4
Z_LO = 4
NEAR = 8


def contract(left, right, left_dim, right_dim):
    return lax.dot_general(
        left, right, (((left_dim,), (right_dim,)), ((), ())), preferred_element_type=jnp.float32
    )


def split_columns(enc_ref, out_ref):
    width = out_ref.shape[2] // Z_HI
    for near in range(NEAR):
        for far in range(Z_HI):
            start = (far * NEAR + near) * width
            out_ref[near, :, far * width : (far + 1) * width] = enc_ref[:, start : start + width]


def join_columns(in_ref, out_ref):
    line = in_ref.shape[0] // NEAR
    part = in_ref.shape[1] // 2
    width = 2 * in_ref.shape[2] // Z_HI
    for near in range(NEAR):
        blocks = [in_ref[at * NEAR + near].astype(jnp.float32) for at in range(line)]
        blocks = [jnp.concatenate([block[:part], block[part:]], axis=1) for block in blocks]
        block = jnp.concatenate(blocks, axis=0).astype(jnp.bfloat16)
        for far in range(Z_HI):
            start = (far * NEAR + near) * width
            out_ref[0, :, start : start + width] = block[:, far * width : (far + 1) * width]


def project(enc_ref, weights_ref, kv_ref):
    near, rows, width = enc_ref.shape
    enc = enc_ref[...].reshape(near * rows, width)
    kv = jnp.dot(enc, weights_ref[...], preferred_element_type=jnp.float32)
    kv_ref[...] = kv.reshape(near, rows, kv.shape[1])


def attend(kv_ref, queries_ref, grad_ref, dkv_ref):
    kv = kv_ref[0]
    for near in range(1, kv_ref.shape[0]):
        kv = kv + kv_ref[near]
    kv = kv.astype(jnp.bfloat16)
    head = queries_ref.shape[1]
    scale = 1.0 / head**0.5
    queries = queries_ref[...]
    grad = grad_ref[...]
    scores = contract(kv[:, :head], queries, 1, 1) * scale
    expd = jnp.exp(scores - jnp.max(scores, axis=0, keepdims=True))
    probs = expd / jnp.sum(expd, axis=0, keepdims=True)
    dprobs = contract(kv[:, head:], grad, 1, 1)
    delta = jnp.sum(probs * dprobs, axis=0, keepdims=True)
    dscores = (probs * (dprobs - delta) * scale).astype(jnp.bfloat16)
    dkv_ref[:, :head] = contract(dscores, queries, 1, 0).astype(jnp.bfloat16)
    dkv_ref[:, head:] = contract(probs.astype(jnp.bfloat16), grad, 1, 0).astype(jnp.bfloat16)


def spread(dkv_ref, weights_ref, out_ref):
    line, piece, width = out_ref.shape
    near, rows, both = dkv_ref.shape
    part = rows // line
    dkv = dkv_ref[...].astype(jnp.float32)
    dkv = [dkv[:, at * part : (at + 1) * part].reshape(piece, both) for at in range(line)]
    dkv = jnp.concatenate(dkv, axis=0).astype(jnp.bfloat16)
    out = contract(dkv, weights_ref[...], 1, 1)
    out_ref[...] = out.astype(jnp.bfloat16).reshape(out_ref.shape)


def weight_terms(place_ref, enc_ref, dkv_ref, own_ref, next_ref, far_ref, last_ref, terms_ref):
    near, rows, width = dkv_ref.shape
    dkv = dkv_ref[...].reshape(near * rows, width)
    enc = enc_ref[...].reshape(near * rows, enc_ref.shape[2])
    terms = contract(enc, dkv, 0, 0)
    depth = own_ref.shape[0]
    for far in range(Z_HI):
        terms_ref[far] = terms[far * depth : (far + 1) * depth]
    for step, ref in enumerate((own_ref, next_ref, far_ref, last_ref)):
        ref[...] = terms_ref[lax.rem(place_ref[0] + step, Z_HI)].astype(ref.dtype)


def row_total(in_ref, out_ref):
    total = in_ref[0].astype(jnp.float32)
    for step in range(1, in_ref.shape[0]):
        total = total + in_ref[step].astype(jnp.float32)
    out_ref[...] = total.astype(jnp.bfloat16)


def suffix_sums(in_ref, one_ref, two_ref, three_ref, out_ref):
    line, piece, width = in_ref.shape
    part = piece // NEAR
    half = width // 2
    total = one_ref[...].astype(jnp.float32) + two_ref[...].astype(jnp.float32) + three_ref[...].astype(jnp.float32)
    for at in range(line - 1, -1, -1):
        total = total + in_ref[at].astype(jnp.float32)
        left = total[:, :half].reshape(NEAR, part, half)
        right = total[:, half:].reshape(NEAR, part, half)
        out_ref[at * NEAR : (at + 1) * NEAR] = jnp.concatenate([left, right], axis=1).astype(jnp.bfloat16)


def add_terms(own_ref, *refs):
    total = own_ref[...]
    for ref in refs[:-1]:
        total = total + ref[...].astype(jnp.float32)
    refs[-1][...] = total.astype(refs[-1].dtype)


def call(kernel, outs, args, flops=0, scalars=0, scratch=()):
    outs = [jax.ShapeDtypeStruct(shape, dtype) for shape, dtype in outs]
    vmem = pl.BlockSpec(memory_space=pltpu.VMEM)
    smem = pl.BlockSpec(memory_space=pltpu.SMEM)
    moved = sum(a.size * a.dtype.itemsize for a in [*args, *outs])
    results = pl.pallas_call(
        kernel,
        out_shape=outs,
        in_specs=[smem] * scalars + [vmem] * (len(args) - scalars),
        out_specs=[vmem] * len(outs),
        scratch_shapes=scratch,
        cost_estimate=pl.CostEstimate(flops=flops, bytes_accessed=moved, transcendentals=0),
        compiler_params=pltpu.CompilerParams(vmem_limit_bytes=24 << 20),
    )(*args)
    return results[0] if len(outs) == 1 else results


def shards(enc_out, kv_weight, queries, out_grad):
    rows, model = enc_out.shape
    depth, both = kv_weight.shape[1:]
    sections = lax.axis_size("section")
    line = sections // Z_LO
    width = Z_HI * depth
    low, high = jnp.bfloat16, jnp.float32
    near_groups = [[far * NEAR + near for near in range(NEAR)] for far in range(Z_HI)]
    far_groups = [[far * NEAR + near for far in range(Z_HI)] for near in range(NEAR)]
    place = lax.div(lax.axis_index("dp"), NEAR).astype(jnp.int32).reshape(1)
    work = 2 * NEAR * rows * width * both

    def shifted(array, step):
        pairs = [
            (far * NEAR + near, (far + step) % Z_HI * NEAR + near) for far in range(Z_HI) for near in range(NEAR)
        ]
        return lax.ppermute(array, "dp", pairs)

    def passed(array, step, ups):
        pairs = [
            (
                ((up * line + at) * Z_HI + far) * NEAR + near,
                ((up * line + at) * Z_HI + (far + step) % Z_HI) * NEAR + near,
            )
            for up in ups
            for at in range(line)
            for far in range(Z_HI)
            for near in range(NEAR)
        ]
        return lax.ppermute(array, ("section", "dp"), pairs)

    def exchange(array, axis, groups=None):
        return lax.all_to_all(array, axis, 0, 0, axis_index_groups=groups)

    enc = call(split_columns, [((NEAR, rows, width), low)], [enc_out])
    own, enc = lax.optimization_barrier((kv_weight[0], enc))
    enc = exchange(enc, "dp", near_groups)
    weights = lax.all_gather(own, "dp", axis=0, tiled=True, axis_index_groups=far_groups)
    kv = call(project, [((NEAR, rows, both), high)], [enc, weights], flops=work)
    kv = exchange(kv, "dp", near_groups)
    dkv = call(attend, [((rows, both), low)], [kv, queries[0], out_grad[0]], flops=8 * rows * queries.size)
    dkv = exchange(jnp.broadcast_to(dkv[None], (NEAR, rows, both)), "dp", near_groups)
    line_groups = [[up * line + step for step in range(line)] for up in range(Z_LO)]
    piece = NEAR * rows // line
    plane_groups = [
        [((up * line + at) * Z_HI + far) * NEAR + near for at in range(line) for near in range(NEAR)]
        for up in range(Z_LO)
        for far in range(Z_HI)
    ]

    def lowered(array, step):
        pairs = [(up * line + at, (up - step) * line + at) for up in range(step, Z_LO) for at in range(line)]
        return lax.ppermute(array, "section", pairs)

    part = call(spread, [((line, piece, width), low)], [dkv, weights], flops=work)
    part, dkv = lax.optimization_barrier((part, dkv))
    part = exchange(part, "section", line_groups)
    mine, after, beyond, before = call(
        weight_terms,
        [((depth, both), high)] * 2 + [((depth, both), low)] * 2,
        [place, enc, dkv],
        flops=work,
        scalars=1,
        scratch=[pltpu.VMEM((Z_HI, depth, both), high)],
    )
    beyond = shifted(beyond, 1)
    after = call(add_terms, [((depth, both), low)], [after, beyond])
    low_after, high_after = passed(after, 1, range(3)), passed(after, 1, range(3, Z_LO))
    low_before, high_before = passed(before, -1, range(2)), passed(before, -1, range(2, Z_LO))
    total = call(row_total, [((piece, width), low)], [part])
    above = [lowered(total, step) for step in (2, 3, 1)]
    above, beyond = lax.optimization_barrier((above, beyond))
    sums = call(suffix_sums, [((line * NEAR, 2 * piece // NEAR, width // 2), low)], [part, *above])
    sums = exchange(sums, ("section", "dp"), plane_groups)
    mine = call(add_terms, [((depth, both), high)], [mine, low_after, high_before], flops=int(4e9))
    sums, mine = lax.optimization_barrier((sums, mine))
    enc_grad = call(join_columns, [((1, rows, model), low)], [sums])
    enc_grad, mine, high_after, low_before = lax.optimization_barrier((enc_grad, mine, high_after, low_before))
    weight_grad = call(add_terms, [((depth, both), high)], [mine, high_after, low_before])[None]
    return enc_grad, weight_grad


def solution(mesh):
    in_specs = (
        P("dp", None),
        P("section", "dp", None),
        P("section", "dp", None),
        P("section", "dp", None),
    )
    out_specs = (P("section", "dp", None), P("section", "dp", None))
    return jax.shard_map(shards, mesh=mesh, in_specs=in_specs, out_specs=out_specs, check_vma=False)
```

```python
import jax
import jax.numpy as jnp
from jax import lax
from jax.experimental import pallas as pl
from jax.experimental.pallas import tpu as pltpu
from jax.sharding import PartitionSpec as P

Z_HI = 4
Z_LO = 4
NEAR = 8


def contract(left, right, left_dim, right_dim):
    return lax.dot_general(
        left, right, (((left_dim,), (right_dim,)), ((), ())), preferred_element_type=jnp.float32
    )


def split_columns(enc_ref, out_ref):
    width = out_ref.shape[2] // Z_HI
    for near in range(NEAR):
        for far in range(Z_HI):
            start = (far * NEAR + near) * width
            out_ref[near, :, far * width : (far + 1) * width] = enc_ref[:, start : start + width]


def join_columns(in_ref, out_ref):
    line = in_ref.shape[0] // NEAR
    part = in_ref.shape[1] // 2
    width = 2 * in_ref.shape[2] // Z_HI
    for near in range(NEAR):
        blocks = [in_ref[at * NEAR + near].astype(jnp.float32) for at in range(line)]
        blocks = [jnp.concatenate([block[:part], block[part:]], axis=1) for block in blocks]
        block = jnp.concatenate(blocks, axis=0).astype(jnp.bfloat16)
        for far in range(Z_HI):
            start = (far * NEAR + near) * width
            out_ref[0, :, start : start + width] = block[:, far * width : (far + 1) * width]


def project(enc_ref, weights_ref, kv_ref):
    near, rows, width = enc_ref.shape
    enc = enc_ref[...].reshape(near * rows, width)
    kv = jnp.dot(enc, weights_ref[...], preferred_element_type=jnp.float32)
    kv_ref[...] = kv.reshape(near, rows, kv.shape[1])


def attend(kv_ref, queries_ref, grad_ref, dkv_ref):
    kv = kv_ref[0]
    for near in range(1, kv_ref.shape[0]):
        kv = kv + kv_ref[near]
    kv = kv.astype(jnp.bfloat16)
    head = queries_ref.shape[1]
    scale = 1.0 / head**0.5
    queries = queries_ref[...]
    grad = grad_ref[...]
    scores = contract(kv[:, :head], queries, 1, 1) * scale
    expd = jnp.exp(scores - jnp.max(scores, axis=0, keepdims=True))
    probs = expd / jnp.sum(expd, axis=0, keepdims=True)
    dprobs = contract(kv[:, head:], grad, 1, 1)
    delta = jnp.sum(probs * dprobs, axis=0, keepdims=True)
    dscores = (probs * (dprobs - delta) * scale).astype(jnp.bfloat16)
    dkv_ref[:, :head] = contract(dscores, queries, 1, 0).astype(jnp.bfloat16)
    dkv_ref[:, head:] = contract(probs.astype(jnp.bfloat16), grad, 1, 0).astype(jnp.bfloat16)


def spread(dkv_ref, weights_ref, out_ref):
    line, piece, width = out_ref.shape
    near, rows, both = dkv_ref.shape
    part = rows // line
    dkv = dkv_ref[...].astype(jnp.float32)
    dkv = [dkv[:, at * part : (at + 1) * part].reshape(piece, both) for at in range(line)]
    dkv = jnp.concatenate(dkv, axis=0).astype(jnp.bfloat16)
    out = contract(dkv, weights_ref[...], 1, 1)
    out_ref[...] = out.astype(jnp.bfloat16).reshape(out_ref.shape)


def weight_terms(place_ref, enc_ref, dkv_ref, own_ref, next_ref, far_ref, last_ref, terms_ref):
    near, rows, width = dkv_ref.shape
    dkv = dkv_ref[...].reshape(near * rows, width)
    enc = enc_ref[...].reshape(near * rows, enc_ref.shape[2])
    terms = contract(enc, dkv, 0, 0)
    depth = own_ref.shape[0]
    for far in range(Z_HI):
        terms_ref[far] = terms[far * depth : (far + 1) * depth]
    for step, ref in enumerate((own_ref, next_ref, far_ref, last_ref)):
        ref[...] = terms_ref[lax.rem(place_ref[0] + step, Z_HI)].astype(ref.dtype)


def row_total(in_ref, out_ref):
    total = in_ref[0].astype(jnp.float32)
    for step in range(1, in_ref.shape[0]):
        total = total + in_ref[step].astype(jnp.float32)
    out_ref[...] = total.astype(jnp.bfloat16)


def suffix_sums(in_ref, one_ref, two_ref, three_ref, out_ref):
    line, piece, width = in_ref.shape
    part = piece // NEAR
    half = width // 2
    total = one_ref[...].astype(jnp.float32) + two_ref[...].astype(jnp.float32) + three_ref[...].astype(jnp.float32)
    for at in range(line - 1, -1, -1):
        total = total + in_ref[at].astype(jnp.float32)
        left = total[:, :half].reshape(NEAR, part, half)
        right = total[:, half:].reshape(NEAR, part, half)
        out_ref[at * NEAR : (at + 1) * NEAR] = jnp.concatenate([left, right], axis=1).astype(jnp.bfloat16)


def add_terms(own_ref, *refs):
    total = own_ref[...]
    for ref in refs[:-1]:
        total = total + ref[...].astype(jnp.float32)
    refs[-1][...] = total.astype(refs[-1].dtype)


def finish(sums_ref, own_ref, last_ref, enc_grad_ref, weight_grad_ref):
    join_columns(sums_ref, enc_grad_ref)
    weight_grad_ref[0] = own_ref[...] + last_ref[...].astype(jnp.float32)


def call(kernel, outs, args, flops=0, scalars=0, scratch=()):
    outs = [jax.ShapeDtypeStruct(shape, dtype) for shape, dtype in outs]
    vmem = pl.BlockSpec(memory_space=pltpu.VMEM)
    smem = pl.BlockSpec(memory_space=pltpu.SMEM)
    moved = sum(a.size * a.dtype.itemsize for a in [*args, *outs])
    results = pl.pallas_call(
        kernel,
        out_shape=outs,
        in_specs=[smem] * scalars + [vmem] * (len(args) - scalars),
        out_specs=[vmem] * len(outs),
        scratch_shapes=scratch,
        cost_estimate=pl.CostEstimate(flops=flops, bytes_accessed=moved, transcendentals=0),
        compiler_params=pltpu.CompilerParams(vmem_limit_bytes=24 << 20),
    )(*args)
    return results[0] if len(outs) == 1 else results


def shards(enc_out, kv_weight, queries, out_grad):
    rows, model = enc_out.shape
    depth, both = kv_weight.shape[1:]
    sections = lax.axis_size("section")
    line = sections // Z_LO
    width = Z_HI * depth
    low, high = jnp.bfloat16, jnp.float32
    near_groups = [[far * NEAR + near for near in range(NEAR)] for far in range(Z_HI)]
    far_groups = [[far * NEAR + near for far in range(Z_HI)] for near in range(NEAR)]
    place = lax.div(lax.axis_index("dp"), NEAR).astype(jnp.int32).reshape(1)
    work = 2 * NEAR * rows * width * both

    def shifted(array, step):
        pairs = [
            (far * NEAR + near, (far + step) % Z_HI * NEAR + near) for far in range(Z_HI) for near in range(NEAR)
        ]
        return lax.ppermute(array, "dp", pairs)

    def returned(array, ups):
        pairs = [
            ((up * line + at) * Z_HI * NEAR + far * NEAR + near, (up * line + at) * Z_HI * NEAR + (far - 1) % Z_HI * NEAR + near)
            for up in ups
            for at in range(line)
            for far in range(Z_HI)
            for near in range(NEAR)
        ]
        return lax.ppermute(array, ("section", "dp"), pairs)

    def exchange(array, axis, groups=None):
        return lax.all_to_all(array, axis, 0, 0, axis_index_groups=groups)

    enc = call(split_columns, [((NEAR, rows, width), low)], [enc_out])
    own, enc = lax.optimization_barrier((kv_weight[0], enc))
    enc = exchange(enc, "dp", near_groups)
    weights = lax.all_gather(own, "dp", axis=0, tiled=True, axis_index_groups=far_groups)
    kv = call(project, [((NEAR, rows, both), high)], [enc, weights], flops=work)
    kv = exchange(kv, "dp", near_groups)
    dkv = call(attend, [((rows, both), low)], [kv, queries[0], out_grad[0]], flops=8 * rows * queries.size)
    dkv = exchange(jnp.broadcast_to(dkv[None], (NEAR, rows, both)), "dp", near_groups)
    line_groups = [[up * line + step for step in range(line)] for up in range(Z_LO)]
    piece = NEAR * rows // line
    plane_groups = [
        [((up * line + at) * Z_HI + far) * NEAR + near for at in range(line) for near in range(NEAR)]
        for up in range(Z_LO)
        for far in range(Z_HI)
    ]

    def lowered(array, step):
        pairs = [(up * line + at, (up - step) * line + at) for up in range(step, Z_LO) for at in range(line)]
        return lax.ppermute(array, "section", pairs)

    part = call(spread, [((line, piece, width), low)], [dkv, weights], flops=work)
    part, dkv = lax.optimization_barrier((part, dkv))
    part = exchange(part, "section", line_groups)
    mine, after, beyond, before = call(
        weight_terms,
        [((depth, both), high)] * 2 + [((depth, both), low)] * 2,
        [place, enc, dkv],
        flops=work,
        scalars=1,
        scratch=[pltpu.VMEM((Z_HI, depth, both), high)],
    )
    beyond = shifted(beyond, 1)
    after = shifted(call(add_terms, [((depth, both), low)], [after, beyond]), 1)
    lower, upper = returned(before, range(Z_LO // 2)), returned(before, range(Z_LO // 2, Z_LO))
    total = call(row_total, [((piece, width), low)], [part])
    above = [lowered(total, step) for step in (2,3,1)]
    above, beyond = lax.optimization_barrier((above, beyond))
    sums = call(suffix_sums, [((line * NEAR, 2 * piece // NEAR, width // 2), low)], [part, *above])
    sums = exchange(sums, ("section", "dp"), plane_groups)
    mine = call(add_terms, [((depth, both), high)], [mine, after, upper], flops=int(4e9))
    sums, mine = lax.optimization_barrier((sums, mine))
    enc_grad, weight_grad = call(
        finish, [((1, rows, model), low), ((1, depth, both), high)], [sums, mine, lower]
    )
    return enc_grad, weight_grad


def solution(mesh):
    in_specs = (
        P("dp", None),
        P("section", "dp", None),
        P("section", "dp", None),
        P("section", "dp", None),
    )
    out_specs = (P("section", "dp", None), P("section", "dp", None))
    return jax.shard_map(shards, mesh=mesh, in_specs=in_specs, out_specs=out_specs, check_vma=False)
```
